32 devices in a mesh: inj: 4 (over y, x), blk: 8 (over z, core).
Axes of the slice: x: 2, y: 2, z: 4, core: 2. Of those that a mesh axis runs over, the one named last changes fastest.
Arguments:
- tile_values: bfloat16 [96, 128, 128], P('blk'), may hold values from -0.3125 to 0.3125
- tile_row: int32 [96], P('blk'), may hold values from 0 to 3
- tile_dest: int32 [96, 1], P('blk'), may hold values from 0 to 6, as said below
- trans_block: int32 [8, 21], P('blk'), may hold values from 0 to 3
- inj_pores: int32 [256, 512], P('inj', 'blk'), may hold values from 0 to 511
- final_weight: bfloat16 [256, 4096], P('inj', 'blk'), may hold values from -6 to 6
Outputs:
- sensitivity: bfloat16 [256, 4096], P('inj', 'blk')
- tile_gradient: bfloat16 [96, 128, 128], P('blk', 'inj')
The draws below stay inside these ranges and needn't reach their ends.
Inputs may be any that keep to these rules, and one draw needn't show every extreme that they name: `tile_dest`: among the tiles of one index of blk, every value is named by at most 3 tiles, and 0 by exactly 3 tiles.
All inputs are finite; a program needn't handle non-finite values.
Results may differ from the reference program's by a relative error of at most 0.014.
Values may be sent and summed in bfloat16 or wider, within the bound.
No kernel may reach another device: no remote copies, remote signals or barrier semaphores. Data moves between devices by JAX's collectives and lax.ppermute only.
A program may use at most 64 MiB of HBM per device.

```python
import math
import jax
import jax.numpy as jnp
import numpy as np
from jax import lax

BW = 128
SET_DEV = 64
DEG = 3
NEIGH = 6
STEPS = 4
BLK_DEV = 4
TILE_DEV = 12
CAP = 3
PORES_DEV = 512
INJ_DEV = 64
NB = 32
PORES = 4096
TILES = 96
SETS = 256
N_INJ = 4
N_BLK = 8


def draw_tile_dest(key, part):

    def one_device(sub):
        first_key, second_key = jax.random.split(sub)
        order = jax.random.permutation(first_key, NEIGH * CAP).astype(jnp.int32)
        chosen = (order[:TILE_DEV - CAP] // CAP + 1).astype(jnp.int32)
        labels = jnp.concatenate([jnp.zeros((CAP,), jnp.int32), chosen])
        return jax.random.permutation(second_key, labels).astype(jnp.int32)
    keys = jax.random.split(jax.random.fold_in(key, 7), N_BLK)
    return jax.vmap(one_device)(keys).reshape(TILES, 1).astype(jnp.int32)


def with_ends(entries, stream_key, least, high):
    dims = entries.shape
    place = [jax.random.randint(jax.random.fold_in(stream_key, axis), (), 0, dims[axis]) for axis in range(len(dims))]
    entries = entries.at[tuple(place)].set(least)
    longest = dims.index(max(dims))
    place[longest] = (place[longest] + 1) % dims[longest]
    return entries.at[tuple(place)].set(high)


def levels(rng, dims, cuts, smallest, top_value):
    gain = 1.0
    for axis_at, shards_of in cuts:
        heights = jax.random.uniform(jax.random.fold_in(jax.random.fold_in(rng, 6), axis_at), (shards_of,), jnp.float32, smallest / len(cuts), top_value / len(cuts))
        gain = gain * jnp.repeat(jnp.exp(heights), dims[axis_at] // shards_of).reshape((-1,) + (1,) * (len(dims) - 1 - axis_at))
    return gain


def rank_table(number_of, skew):
    portions = [(1 << 20) // math.isqrt(rank ** skew) + 1 for rank in range(1, number_of + 1)]
    spread = 1 + sum(portions) // (1 << 30)
    return np.cumsum(np.array([max(1, weight // spread) for weight in portions]))


def ranked_ids(rng, shape, count, lean):
    grid = rank_table(count, lean)
    pick = jax.random.randint(jax.random.fold_in(rng, 1), shape, 0, int(grid[count - 1]))
    rank = jnp.searchsorted(jnp.asarray(grid, jnp.int32), pick, side="right")
    return jax.random.permutation(jax.random.fold_in(rng, 2), count)[rank].astype(jnp.int32)


def noise(rng, dims, spread, reach, shards=(), held_as=jnp.bfloat16):
    drawn = spread * jax.random.normal(rng, dims, jnp.float32)
    if shards:
        drawn = drawn * levels(rng, dims, shards, -0.22, 0.18)
    return jnp.clip(drawn, -reach, reach).astype(held_as)


def setup_inputs(seed: int = 0) -> dict:
    seeds = jax.random.split(jax.random.key(seed), 7)
    return {
        "tile_values": noise(seeds[0], (TILES, BW, BW), (DEG * BW) ** -0.5, 0.3125, ((0, 8),)),
        "tile_row": with_ends(ranked_ids(seeds[1], (TILES,), BLK_DEV, 2), jax.random.fold_in(seeds[1], 3), 0, BLK_DEV - 1).astype(jnp.int32),
        "tile_dest": draw_tile_dest(jax.random.fold_in(seeds[6], 71), 0),
        "trans_block": with_ends(jax.random.randint(seeds[3], (N_BLK, (NEIGH + 1) * CAP), 0, BLK_DEV), jax.random.fold_in(seeds[3], 1), 0, BLK_DEV - 1).astype(jnp.int32),
        "inj_pores": with_ends(jax.random.randint(seeds[4], (SETS, INJ_DEV * N_BLK), 0, PORES_DEV), jax.random.fold_in(seeds[4], 1), 0, PORES_DEV - 1).astype(jnp.int32),
        "final_weight": noise(seeds[5], (SETS, PORES), 1.0, 6.0, ((0, 4), (1, 8))),
    }


def reference(tile_values, tile_row, tile_dest, trans_block, inj_pores, final_weight):
    highest = lax.Precision.HIGHEST
    slot_ids = jnp.arange(NEIGH + 1, dtype=jnp.int32)
    half_ids = ((slot_ids + 1) // 2).astype(jnp.int32)
    offsets = jnp.where(slot_ids % 2 == 1, half_ids, -half_ids).astype(jnp.int32)
    targets = tile_dest.reshape(N_BLK, TILE_DEV).astype(jnp.int32)
    rows_local = tile_row.reshape(N_BLK, TILE_DEV).astype(jnp.int32)
    ordinal = jnp.arange(TILE_DEV, dtype=jnp.int32)
    earlier = ordinal[:, None] > ordinal[None, :]
    position = jnp.sum(((targets[:, :, None] == targets[:, None, :]) & earlier[None]).astype(jnp.int32), axis=2).astype(jnp.int32)
    owners = jnp.arange(N_BLK, dtype=jnp.int32)[:, None]
    dest_dev = ((owners + offsets[targets]) % N_BLK).astype(jnp.int32)
    local_col = trans_block[dest_dev, targets * CAP + position].astype(jnp.int32)
    col_glob = (dest_dev * BLK_DEV + local_col).astype(jnp.int32)
    row_glob = (owners * BLK_DEV + rows_local).astype(jnp.int32)
    tiles = tile_values.reshape(N_BLK, TILE_DEV, BW, BW)

    entry_dev = (jnp.arange(INJ_DEV * N_BLK, dtype=jnp.int32) // INJ_DEV).astype(jnp.int32)
    pore_ids = (entry_dev[None, :] * PORES_DEV + inj_pores).astype(jnp.int32)
    set_ids = jnp.arange(SETS, dtype=jnp.int32)[:, None]
    initial = jnp.zeros((SETS, PORES), jnp.float32).at[set_ids, pore_ids].add(1.0)
    initial = initial.astype(jnp.bfloat16).reshape(SETS, NB, BW)

    def advance(state):
        def one_device(pieces):
            tile_set, row_set, col_set = pieces
            fetched = state[:, col_set].astype(jnp.float32)
            contrib = jnp.einsum("sib,iab->sia", fetched, tile_set.astype(jnp.float32), precision=highest)
            row_hot = (row_set[:, None] == jnp.arange(BLK_DEV, dtype=jnp.int32)[None, :]).astype(jnp.float32)
            return jnp.einsum("sia,ic->sca", contrib, row_hot, precision=highest).astype(jnp.bfloat16)
        result = lax.map(one_device, (tiles, rows_local, col_glob))
        return jnp.transpose(result, (1, 0, 2, 3)).reshape(SETS, NB, BW)

    states = [initial]
    for timestep in range(STEPS - 1):
        states.append(advance(states[-1]))

    def retreat(adjoint):
        def add_device(total, pieces):
            tile_set, row_set, col_set = pieces
            rows_now = adjoint[:, row_set].astype(jnp.float32)
            term = jnp.einsum("sia,iab->sib", rows_now, tile_set.astype(jnp.float32), precision=highest)
            term = lax.optimization_barrier(term.astype(jnp.bfloat16)).astype(jnp.float32)
            return total.at[:, col_set].add(term), None
        total, unused = lax.scan(add_device, jnp.zeros((SETS, NB, BW), jnp.float32), (tiles, row_glob, col_glob))
        return total.astype(jnp.bfloat16)

    adjoints = [None] * (STEPS + 1)
    adjoints[STEPS] = final_weight.reshape(SETS, NB, BW)
    for timestep in reversed(range(STEPS)):
        adjoints[timestep] = retreat(adjoints[timestep + 1])

    def grad_device(pieces):
        row_set, col_set = pieces
        accum = jnp.zeros((N_INJ, TILE_DEV, BW, BW), jnp.float32)
        for timestep in range(STEPS):
            rows_now = adjoints[timestep + 1][:, row_set].astype(jnp.float32).reshape(N_INJ, SET_DEV, TILE_DEV, BW)
            cols_now = states[timestep][:, col_set].astype(jnp.float32).reshape(N_INJ, SET_DEV, TILE_DEV, BW)
            accum = accum + jnp.einsum("gsia,gsib->giab", rows_now, cols_now, precision=highest)
        partial_sum = lax.optimization_barrier((accum * (1.0 / SET_DEV)).astype(jnp.bfloat16)).astype(jnp.float32)
        return jnp.sum(partial_sum, axis=0).astype(jnp.bfloat16)

    tile_gradient = lax.map(grad_device, (row_glob, col_glob)).reshape(TILES, BW, BW)
    sensitivity = adjoints[0].reshape(SETS, PORES)
    return (sensitivity, tile_gradient)
```

```python
import functools

import jax
import jax.numpy as jnp
from jax import lax
from jax.experimental import pallas as pl
from jax.experimental.pallas import tpu as pltpu
from jax.sharding import PartitionSpec as P

NEIGH = 6
STEPS = 4
F32, BF16, I32 = jnp.float32, jnp.bfloat16, jnp.int32


def pair_shift(block, amount):
    count = lax.axis_size("blk")
    return lax.ppermute(block, "blk", [(i, (i + 2 * amount) % count) for i in range(count)])


def pair_swap(block):
    return lax.ppermute(block, "blk", [(i, i ^ 1) for i in range(lax.axis_size("blk"))])


def far_pairs(upward, downward):
    if lax.axis_size("blk") == 8:
        both = pair_shift(jnp.concatenate([upward, downward]), 2)
        return both[: upward.shape[0]], both[upward.shape[0] :]
    return pair_shift(upward, 2), pair_shift(downward, -2)


def vmem():
    return pl.BlockSpec(memory_space=pltpu.VMEM)


def smem():
    return pl.BlockSpec(memory_space=pltpu.SMEM)


def call(body, ints, arrays, outs, scratch=()):
    return pl.pallas_call(
        body,
        out_shape=outs,
        in_specs=[smem()] * len(ints) + [vmem()] * len(arrays),
        out_specs=[vmem()] * len(outs),
        scratch_shapes=list(scratch),
        compiler_params=pltpu.CompilerParams(vmem_limit_bytes=32 * 1024 * 1024),
    )(*ints, *arrays)


def shape(rows, width, kind=BF16):
    return jax.ShapeDtypeStruct((rows, width), kind)


def blocks(start, sets, count=1):
    return pl.ds(pl.multiple_of(start * sets, sets), sets * count)


def split_kernel(width, place_ref, pores_ref, weight_ref, keep_ref, send_ref):
    core = place_ref[0]
    sets = pores_ref.shape[0] // 2
    entries = pores_ref.shape[1]
    count = weight_ref.shape[1] // width
    lane = lax.broadcasted_iota(I32, (sets, width), 1)
    for half, out_ref in ((core, keep_ref), (1 - core, send_ref)):
        rows = pl.ds(pl.multiple_of(half * sets, sets), sets)
        pores = pores_ref[rows, :]
        totals = [jnp.zeros((sets, width), F32) for _ in range(count)]
        for entry in range(entries):
            pore = pores[:, entry : entry + 1]
            for block in range(count):
                totals[block] += jnp.where(pore == lane + block * width, 1.0, 0.0)
        for block in range(count):
            out_ref[block * sets : (block + 1) * sets, :] = totals[block].astype(BF16)
            out_ref[(count + block) * sets : (count + block + 1) * sets, :] = weight_ref[
                rows, block * width : (block + 1) * width
            ]


def start_kernel(sets, count, ints_ref, keep_ref, recv_ref, table_ref, state_ref, weight_ref, up_ref, down_ref):
    core = ints_ref[0]
    part = count * sets
    mine = pl.ds(pl.multiple_of(core * part, part), part)
    other = pl.ds(pl.multiple_of((1 - core) * part, part), part)
    state_ref[mine, :] = keep_ref[:part, :]
    state_ref[other, :] = recv_ref[:part, :]
    state_ref[2 * part :, :] = table_ref[...]
    weight_ref[mine, :] = keep_ref[part:, :]
    weight_ref[other, :] = recv_ref[part:, :]
    pick_far(sets, ints_ref, 1, state_ref, up_ref, down_ref)


def pick_far(sets, ints_ref, at, state_ref, up_ref, down_ref):
    capacity = up_ref.shape[0] // sets
    for k in range(capacity):
        up_ref[k * sets : (k + 1) * sets, :] = state_ref[blocks(ints_ref[at + k], sets), :]
        down_ref[k * sets : (k + 1) * sets, :] = state_ref[blocks(ints_ref[at + capacity + k], sets), :]


def fill(near, far, own_ref, above_ref, below_ref, low_ref, high_ref, into_ref):
    into_ref[:near, :] = own_ref[:near, :]
    into_ref[near : 2 * near, :] = above_ref[:near, :]
    into_ref[2 * near : 3 * near, :] = below_ref[:near, :]
    into_ref[3 * near : 3 * near + far, :] = low_ref[...]
    into_ref[3 * near + far :, :] = high_ref[...]


def forward_kernel(
    sets, far_at, ints_ref, own_ref, above_ref, below_ref, low_ref, high_ref, mine_ref, other_ref,
    state_ref, up_ref, down_ref, columns_ref, seen_ref, total_ref,
):
    tiles = mine_ref.shape[0]
    fill(state_ref.shape[0], low_ref.shape[0], own_ref, above_ref, below_ref, low_ref, high_ref, seen_ref)
    total_ref[...] = jnp.zeros_like(total_ref)
    for i in range(2 * tiles):
        tile = mine_ref[i] if i < tiles else other_ref[i - tiles]
        column = seen_ref[blocks(ints_ref[i], sets), :]
        columns_ref[i * sets : (i + 1) * sets, :] = column
        rows = blocks(ints_ref[2 * tiles + i], sets)
        total_ref[rows, :] += lax.dot_general(column, tile, (((1,), (1,)), ((), ())), preferred_element_type=F32)
    state_ref[...] = total_ref[...].astype(BF16)
    pick_far(sets, ints_ref, far_at, state_ref, up_ref, down_ref)


def terms(sets, ints_ref, adjoint_ref, mine_ref, other_ref, total_ref):
    tiles = mine_ref.shape[0]
    total_ref[...] = jnp.zeros_like(total_ref)
    for i in range(2 * tiles):
        tile = mine_ref[i] if i < tiles else other_ref[i - tiles]
        row = adjoint_ref[blocks(ints_ref[2 * tiles + i], sets), :]
        total_ref[blocks(ints_ref[i], sets), :] += jnp.dot(row, tile, preferred_element_type=F32)


def post(total_ref, own_ref, above_ref, below_ref, low_ref, high_ref):
    near, far = own_ref.shape[0], low_ref.shape[0]
    own_ref[...] = total_ref[:near, :]
    above_ref[...] = total_ref[near : 2 * near, :].astype(BF16)
    below_ref[...] = total_ref[2 * near : 3 * near, :].astype(BF16)
    low_ref[...] = total_ref[3 * near : 3 * near + far, :].astype(BF16)
    high_ref[...] = total_ref[3 * near + far :, :].astype(BF16)


def collect(sets, far_at, ints_ref, own_ref, above_ref, below_ref, low_ref, high_ref, sum_ref):
    sum_ref[...] = own_ref[...] + above_ref[...].astype(F32) + below_ref[...].astype(F32)
    capacity = low_ref.shape[0] // sets
    for k in range(capacity):
        part = slice(k * sets, (k + 1) * sets)
        sum_ref[blocks(ints_ref[far_at + k], sets), :] += high_ref[part, :].astype(F32)
        sum_ref[blocks(ints_ref[far_at + capacity + k], sets), :] += low_ref[part, :].astype(F32)


def first_terms_kernel(sets, ints_ref, weight_ref, mine_ref, other_ref, *rest):
    *out_refs, total_ref = rest
    terms(sets, ints_ref, weight_ref, mine_ref, other_ref, total_ref)
    post(total_ref, *out_refs)


def adjoint_kernel(sets, far_at, ints_ref, *refs):
    arrived, (mine_ref, other_ref, adjoint_ref), rest = refs[:5], refs[5:8], refs[8:]
    *out_refs, total_ref, sum_ref = rest
    collect(sets, far_at, ints_ref, *arrived, sum_ref)
    adjoint_ref[...] = sum_ref[...].astype(BF16)
    terms(sets, ints_ref, adjoint_ref, mine_ref, other_ref, total_ref)
    post(total_ref, *out_refs)


def last_kernel(sets, far_at, ints_ref, *refs):
    arrived, (keep_ref, send_ref, sum_ref) = refs[:5], refs[5:]
    collect(sets, far_at, ints_ref, *arrived, sum_ref)
    part = keep_ref.shape[0]
    core = ints_ref[far_at - 1]
    keep_ref[...] = sum_ref[pl.ds(pl.multiple_of(core * part, part), part), :].astype(BF16)
    send_ref[...] = sum_ref[pl.ds(pl.multiple_of((1 - core) * part, part), part), :].astype(BF16)


def place_kernel(sets, place_ref, keep_ref, recv_ref, out_ref):
    core = place_ref[0]
    width = keep_ref.shape[1]
    for half, ref in ((core, keep_ref), (1 - core, recv_ref)):
        rows = pl.ds(pl.multiple_of(half * sets, sets), sets)
        for block in range(keep_ref.shape[0] // sets):
            out_ref[rows, block * width : (block + 1) * width] = ref[block * sets : (block + 1) * sets, :]


def gradient_kernel(
    sets, tiles, ints_ref, own_ref, above_ref, below_ref, low_ref, high_ref, *refs
):
    columns, adjoints = refs[: STEPS - 1], refs[STEPS - 1 : 2 * STEPS - 1]
    mine_ref, other_ref, seen_ref, rows_ref, cols_ref = refs[2 * STEPS - 1 :]
    near = adjoints[0].shape[0]
    scale = 1.0 / (2 * sets)
    fill(near, low_ref.shape[0], own_ref, above_ref, below_ref, low_ref, high_ref, seen_ref)
    for t in range(STEPS):
        for block in range(near // sets):
            rows_ref[block, t * sets : (t + 1) * sets, :] = adjoints[t][block * sets : (block + 1) * sets, :]
    for i in range(2 * tiles):
        for t in range(STEPS - 1):
            cols_ref[t * sets : (t + 1) * sets, :] = columns[t][i * sets : (i + 1) * sets, :]
        cols_ref[(STEPS - 1) * sets :, :] = seen_ref[blocks(ints_ref[i], sets), :]
        product = lax.dot_general(
            rows_ref[ints_ref[2 * tiles + i]], cols_ref[...], (((0,), (0,)), ((), ())), preferred_element_type=F32
        )
        if i < tiles:
            mine_ref[i] = product * scale
        else:
            other_ref[i - tiles] = (product * scale).astype(BF16)


def portions_kernel(portion, place_ref, mine_ref, recv_ref, *out_refs):
    place, groups = place_ref[1], len(out_refs)
    for distance, out_ref in enumerate(out_refs):
        to = lax.rem(place + distance, groups)
        rows = pl.ds(pl.multiple_of(to * portion, portion), portion)
        total = mine_ref[:, rows, :] + recv_ref[:, rows, :].astype(F32)
        out_ref[...] = total.astype(out_ref.dtype)


def offset_of(slot):
    amount = (slot + 1) // 2
    return amount if slot % 2 == 1 else -amount


def shards(tile_values, tile_row, tile_dest, trans_block, inj_pores, final_weight):
    tiles, width = tile_values.shape[:2]
    sets = final_weight.shape[0] // 2
    count = final_weight.shape[1] // width
    slots = trans_block.shape[1]
    capacity = slots // (NEIGH + 1)
    near, far = 2 * count * sets, capacity * sets
    core = lax.rem(lax.axis_index("blk"), 2).astype(I32)
    place = jnp.stack([core, lax.axis_index("inj").astype(I32)])

    other_values = pair_swap(tile_values)
    numbers = jnp.concatenate([tile_row, tile_dest[:, 0], trans_block[0]])
    other_numbers = pair_swap(numbers[None, :])[0]
    keep, send = call(
        functools.partial(split_kernel, width), [place], [inj_pores, final_weight],
        [shape(near, width), shape(near, width)],
    )
    recv = pair_swap(send)

    both = jnp.stack([numbers, other_numbers])
    both_rows, both_targets = both[:, :tiles], both[:, tiles : 2 * tiles]
    owner = jnp.stack([core, 1 - core])[:, None]
    mine_table, other_table = both[0, 2 * tiles :], both[1, 2 * tiles :]
    table = jnp.where(core == 0, jnp.stack([mine_table, other_table]), jnp.stack([other_table, mine_table]))
    far_blocks = jnp.concatenate([table[1, 6 * capacity :] + count, table[0, 5 * capacity : 6 * capacity]])
    pad = 16 * width - 2 * slots
    sent_table = jnp.pad(table.reshape(-1).astype(BF16), (0, pad)).reshape(16, width)
    state, weight, up, down = call(
        functools.partial(start_kernel, sets, count), [jnp.concatenate([core[None], far_blocks])],
        [keep, recv, sent_table],
        [shape(near + 16, width), shape(near, width), shape(far, width), shape(far, width)],
    )

    def fetch(state, up, down):
        low, high = far_pairs(up, down)
        return pair_shift(state, -1), pair_shift(state, 1), low, high

    arrived = fetch(state, up, down)

    ordinal = jnp.arange(tiles, dtype=I32)
    earlier = ordinal[:, None] > ordinal[None, :]
    same = both_targets[:, :, None] == both_targets[:, None, :]
    position = jnp.sum((same & earlier[None]).astype(I32), axis=2)
    half = (both_targets + 1) // 2
    offset = jnp.where(both_targets % 2 == 1, half, -half)
    reach = owner + offset
    pair_off = (reach + 4) // 2 - 2
    parity = reach - 2 * pair_off
    source = jnp.where(pair_off == -1, 2, pair_off)
    lookup = (source * 2 + parity) * slots + both_targets * capacity + position
    tables = jnp.concatenate(
        [table.reshape(-1)] + [block[near : near + 1, : 2 * slots].reshape(-1).astype(I32) for block in arrived[:2]]
    )
    hit = lookup[:, :, None] == jnp.arange(6 * slots, dtype=I32)
    listed = jnp.sum(jnp.where(hit, tables, 0), axis=2)
    column = jnp.where(
        pair_off == -2,
        6 * count + position,
        jnp.where(pair_off == 2, 6 * count + capacity + position, (source * 2 + parity) * count + listed),
    )
    ints = jnp.concatenate(
        [column.reshape(-1), (owner * count + both_rows).reshape(-1), core[None], far_blocks]
    )
    far_at = 4 * tiles + 1

    seen = pltpu.VMEM((3 * near + 2 * far, width), BF16)
    seen_sum = pltpu.VMEM((3 * near + 2 * far, width), F32)
    own_sum = pltpu.VMEM((near, width), F32)
    messages = [shape(near, width, F32), shape(near, width), shape(near, width), shape(far, width), shape(far, width)]

    def forward(state, arrived):
        return call(
            functools.partial(forward_kernel, sets, far_at), [ints],
            [state, *arrived, tile_values, other_values],
            [shape(near, width), shape(far, width), shape(far, width), shape(2 * tiles * sets, width)],
            [seen, own_sum],
        )

    def give(above, below, low, high):
        from_low, from_high = far_pairs(high, low)
        return pair_shift(below, -1), pair_shift(above, 1), from_low, from_high

    columns, adjoints = [], [weight]
    own, *posted = call(
        functools.partial(first_terms_kernel, sets), [ints], [weight, tile_values, other_values], messages, [seen_sum]
    )
    for _ in range(STEPS - 1):
        given = give(*posted)
        state, up, down, column_blocks = forward(state, arrived)
        columns.append(column_blocks)
        arrived = fetch(state, up, down)
        adjoint, own, *posted = call(
            functools.partial(adjoint_kernel, sets, far_at), [ints], [own, *given, tile_values, other_values],
            [shape(near, width), *messages], [seen_sum, own_sum],
        )
        adjoints.insert(0, adjoint)

    mine, other = call(
        functools.partial(gradient_kernel, sets, tiles), [ints], [state, *arrived, *columns, *adjoints],
        [jax.ShapeDtypeStruct((tiles, width, width), F32), jax.ShapeDtypeStruct((tiles, width, width), BF16)],
        [seen, pltpu.VMEM((2 * count, STEPS * sets, width), BF16), pltpu.VMEM((STEPS * sets, width), BF16)],
    )
    groups = lax.axis_size("inj")
    portion = width // groups
    pieces = call(
        functools.partial(portions_kernel, portion), [place], [mine, pair_swap(other)],
        [jax.ShapeDtypeStruct((tiles, portion, width), F32 if k == 0 else BF16) for k in range(groups)],
    )
    total = pieces[0]
    for distance in range(1, groups):
        route = [(i, (i + distance) % groups) for i in range(groups)]
        total = total + lax.ppermute(pieces[distance], "inj", route).astype(F32)

    given = give(*posted)
    keep, send = call(
        functools.partial(last_kernel, sets, far_at), [ints], [own, *given],
        [shape(near // 2, width), shape(near // 2, width)], [own_sum],
    )
    (sensitivity,) = call(
        functools.partial(place_kernel, sets), [place], [keep, pair_swap(send)],
        [shape(2 * sets, count * width)],
    )
    return sensitivity, total.astype(BF16)


def solution(mesh):
    placed = (
        P("blk", None, None),
        P("blk"),
        P("blk", None),
        P("blk", None),
        P("inj", "blk"),
        P("inj", "blk"),
    )
    return jax.shard_map(
        shards,
        mesh=mesh,
        in_specs=placed,
        out_specs=(P("inj", "blk"), P("blk", "inj", None)),
        check_vma=False,
    )
```

```python
import functools

import jax
import jax.numpy as jnp
from jax import lax
from jax.experimental import pallas as pl
from jax.experimental.pallas import tpu as pltpu
from jax.sharding import PartitionSpec as P

NEIGH = 6
STEPS = 4
F32, BF16, I32 = jnp.float32, jnp.bfloat16, jnp.int32


def pair_shift(block, amount):
    count = lax.axis_size("blk")
    return lax.ppermute(block, "blk", [(i, (i + 2 * amount) % count) for i in range(count)])


def pair_swap(block):
    return lax.ppermute(block, "blk", [(i, i ^ 1) for i in range(lax.axis_size("blk"))])


def far_pairs(upward, downward):
    if lax.axis_size("blk") == 8:
        both = pair_shift(jnp.concatenate([upward, downward]), 2)
        return both[: upward.shape[0]], both[upward.shape[0] :]
    return pair_shift(upward, 2), pair_shift(downward, -2)


def vmem():
    return pl.BlockSpec(memory_space=pltpu.VMEM)


def smem():
    return pl.BlockSpec(memory_space=pltpu.SMEM)


def call(body, ints, arrays, outs, scratch=()):
    return pl.pallas_call(
        body,
        out_shape=outs,
        in_specs=[smem()] * len(ints) + [vmem()] * len(arrays),
        out_specs=[smem() if out.dtype == I32 else vmem() for out in outs],
        scratch_shapes=list(scratch),
        compiler_params=pltpu.CompilerParams(vmem_limit_bytes=32 * 1024 * 1024),
    )(*ints, *arrays)


def shape(rows, width, kind=BF16):
    return jax.ShapeDtypeStruct((rows, width), kind)


def blocks(start, sets, count=1):
    return pl.ds(pl.multiple_of(start * sets, sets), sets * count)


def slot_of(offset):
    return 2 * offset - 1 if offset > 0 else -2 * offset


def read_table(core, mine_ref, other_ref, device, at):
    return jnp.where(core == device, mine_ref[0, at], other_ref[0, at])


def list_far(capacity, count, table_at, core, mine_ref, other_ref):
    return [
        read_table(core, mine_ref, other_ref, device, table_at + slot_of(offset) * capacity + k) + device * count
        for device, offset in ((1, -3), (0, 3))
        for k in range(capacity)
    ]


def count_kernel(
    width, count, capacity, table_at, place_ref, mine_ref, other_ref, pores_ref, recv_ref, table_ref,
    state_ref, up_ref, down_ref, counts_ref,
):
    core = place_ref[0]
    sets, entries = pores_ref.shape[0] // 2, pores_ref.shape[1]
    rows = pl.ds(pl.multiple_of(core * sets, sets), sets)
    own = pores_ref[rows, :] + core * (count * width)
    pores = jnp.concatenate([own, recv_ref[:sets, :] + (1 - core) * (count * width)], axis=1)
    block = lax.div(pores, width)
    place = pores - block * width
    block_ids = lax.broadcasted_iota(I32, (2 * count, 2 * entries), 0)
    place_ids = lax.broadcasted_iota(I32, (width, 2 * entries), 0)
    for one in range(sets):
        row = slice(one, one + 1)
        by_block = jnp.where(block[row, :] == block_ids, 1.0, 0.0).astype(BF16)
        by_place = jnp.where(place[row, :] == place_ids, 1.0, 0.0).astype(BF16)
        counts_ref[:, one, :] = lax.dot_general(
            by_block, by_place, (((1,), (1,)), ((), ())), preferred_element_type=F32
        )
    for k in range(2 * count):
        state_ref[k * sets : (k + 1) * sets, :] = counts_ref[k].astype(BF16)
    state_ref[2 * count * sets :, :] = table_ref[...]
    pick_far(sets, list_far(capacity, count, table_at, core, mine_ref, other_ref), state_ref, up_ref, down_ref)


def pick_far(sets, listed, state_ref, up_ref, down_ref):
    capacity = up_ref.shape[0] // sets
    for k in range(capacity):
        up_ref[k * sets : (k + 1) * sets, :] = state_ref[blocks(listed[k], sets), :]
        down_ref[k * sets : (k + 1) * sets, :] = state_ref[blocks(listed[capacity + k], sets), :]


def fill(near, far, own_ref, above_ref, below_ref, low_ref, high_ref, into_ref):
    into_ref[:near, :] = own_ref[:near, :]
    into_ref[near : 2 * near, :] = above_ref[:near, :]
    into_ref[2 * near : 3 * near, :] = below_ref[:near, :]
    into_ref[3 * near : 3 * near + far, :] = low_ref[...]
    into_ref[3 * near + far :, :] = high_ref[...]


def forward_kernel(
    sets, far_at, ints_ref, own_ref, above_ref, below_ref, low_ref, high_ref, mine_ref, other_ref,
    state_ref, up_ref, down_ref, columns_ref, seen_ref, total_ref,
):
    tiles = mine_ref.shape[0]
    fill(state_ref.shape[0], low_ref.shape[0], own_ref, above_ref, below_ref, low_ref, high_ref, seen_ref)
    total_ref[...] = jnp.zeros_like(total_ref)
    for i in range(2 * tiles):
        tile = mine_ref[i] if i < tiles else other_ref[i - tiles]
        column = seen_ref[blocks(ints_ref[i], sets), :]
        columns_ref[i * sets : (i + 1) * sets, :] = column
        rows = blocks(ints_ref[2 * tiles + i], sets)
        total_ref[rows, :] += lax.dot_general(column, tile, (((1,), (1,)), ((), ())), preferred_element_type=F32)
    state_ref[...] = total_ref[...].astype(BF16)
    far = 2 * up_ref.shape[0] // sets
    pick_far(sets, [ints_ref[far_at + k] for k in range(far)], state_ref, up_ref, down_ref)


def first_forward_kernel(sets, far_at, slots, plan_ref, tables_ref, *refs):
    arrays, ints_ref, rest = refs[:7], refs[7], refs[8:]
    tiles, near = arrays[-1].shape[0], rest[0].shape[0]
    count = near // sets // 2
    for i in range(2 * tiles):
        side, at = plan_ref[i], plan_ref[2 * tiles + i]
        listed = side * count + tables_ref[jnp.minimum(side, 5) * slots + at]
        ints_ref[i] = jnp.where(side == 6, 6 * count + at, listed)
    for k in range(2 * tiles, ints_ref.shape[0]):
        ints_ref[k] = plan_ref[2 * tiles + k]
    forward_kernel(sets, far_at, ints_ref, *arrays, *rest)


def terms(sets, ints_ref, adjoint_ref, mine_ref, other_ref, total_ref):
    tiles = mine_ref.shape[0]
    total_ref[...] = jnp.zeros_like(total_ref)
    for i in range(2 * tiles):
        tile = mine_ref[i] if i < tiles else other_ref[i - tiles]
        row = adjoint_ref[blocks(ints_ref[2 * tiles + i], sets), :]
        total_ref[blocks(ints_ref[i], sets), :] += jnp.dot(row, tile, preferred_element_type=F32)


def post(total_ref, own_ref, *out_refs):
    at = own_ref.shape[0]
    own_ref[...] = total_ref[:at, :]
    for ref in out_refs:
        ref[...] = total_ref[at : at + ref.shape[0], :].astype(BF16)
        at += ref.shape[0]


def collect(sets, far_at, ints_ref, own_ref, above_ref, below_ref, low_ref, high_ref, sum_ref):
    sum_ref[...] = own_ref[...] + above_ref[...].astype(F32) + below_ref[...].astype(F32)
    capacity = low_ref.shape[0] // sets
    for k in range(capacity):
        part = slice(k * sets, (k + 1) * sets)
        sum_ref[blocks(ints_ref[far_at + k], sets), :] += high_ref[part, :].astype(F32)
        sum_ref[blocks(ints_ref[far_at + capacity + k], sets), :] += low_ref[part, :].astype(F32)


def first_terms_kernel(
    sets, table_at, place_ref, listed_ref, arrived_ref, weight_ref, recv_ref, mine_ref, other_ref,
    plan_ref, placed_ref, *rest,
):
    *out_refs, used_ref, ints_ref, total_ref = rest
    core, width, tiles = place_ref[0], placed_ref.shape[1], mine_ref.shape[0]
    count = weight_ref.shape[1] // width
    capacity = out_refs[-1].shape[0] // sets
    rows = pl.ds(pl.multiple_of(core * sets, sets), sets)
    for block in range(count):
        lanes = slice(block * width, (block + 1) * width)
        placed_ref[blocks(core * count + block, sets), :] = weight_ref[rows, lanes]
        placed_ref[blocks((1 - core) * count + block, sets), :] = recv_ref[:, lanes]
    for k in range(2 * (NEIGH + 1)):
        used_ref[k] = 0
    for i in range(2 * tiles):
        mine = i < tiles
        owner, from_ref, at = (core, listed_ref, i) if mine else (1 - core, arrived_ref, i - tiles)
        target = from_ref[0, tiles + at]
        used_at = target + (0 if mine else NEIGH + 1)
        position = used_ref[used_at]
        used_ref[used_at] = position + 1
        half = lax.shift_right_logical(target + 1, 1)
        reach = owner + jnp.where(target & 1 == 1, half, -half)
        pair_off = lax.shift_right_logical(reach + 4, 1) - 2
        parity = reach - 2 * pair_off
        far = (pair_off == 2) | (pair_off == -2)
        far_slot = jnp.where(pair_off == 2, capacity, 0) + position
        source = jnp.where(pair_off == -1, 2, pair_off)
        entry = target * capacity + position
        own = parity * count + read_table(core, listed_ref, arrived_ref, parity, table_at + entry)
        slot = 2 * count + ((source - 1) * 4 + owner * 2 + parity) * capacity + position
        ints_ref[i] = jnp.where(far, 2 * count + 8 * capacity + far_slot, jnp.where(pair_off == 0, own, slot))
        row = owner * count + from_ref[0, at]
        ints_ref[2 * tiles + i] = row
        plan_ref[i] = jnp.where(far, 6, source * 2 + parity)
        plan_ref[2 * tiles + i] = jnp.where(far, far_slot, entry)
        plan_ref[4 * tiles + i] = row
    plan_ref[6 * tiles] = core
    far_blocks = list_far(capacity, count, table_at, core, listed_ref, arrived_ref)
    slot_blocks = [
        read_table(core, listed_ref, arrived_ref, device, table_at + slot_of(2 * side + device - sender) * capacity + k)
        + device * count
        for side in (-1, 1)
        for sender in (0, 1)
        for device in (0, 1)
        for k in range(capacity)
    ]
    for k, block in enumerate(far_blocks + slot_blocks + far_blocks[capacity:] + far_blocks[:capacity]):
        plan_ref[6 * tiles + 1 + k] = block
    terms(sets, ints_ref, placed_ref, mine_ref, other_ref, total_ref)
    post(total_ref, *out_refs)


def slots_adjoint_kernel(sets, slots_at, ints_ref, *refs):
    (own_ref, *arrived), (mine_ref, other_ref, adjoint_ref), rest = refs[:5], refs[5:8], refs[8:]
    *out_refs, total_ref, sum_ref = rest
    sum_ref[...] = own_ref[...]
    at = slots_at
    for ref in arrived:
        for k in range(ref.shape[0] // sets):
            sum_ref[blocks(ints_ref[at], sets), :] += ref[k * sets : (k + 1) * sets, :].astype(F32)
            at += 1
    adjoint_ref[...] = sum_ref[...].astype(BF16)
    terms(sets, ints_ref, adjoint_ref, mine_ref, other_ref, total_ref)
    post(total_ref, *out_refs)


def adjoint_kernel(sets, far_at, ints_ref, *refs):
    arrived, (mine_ref, other_ref, adjoint_ref), rest = refs[:5], refs[5:8], refs[8:]
    *out_refs, total_ref, sum_ref = rest
    collect(sets, far_at, ints_ref, *arrived, sum_ref)
    adjoint_ref[...] = sum_ref[...].astype(BF16)
    terms(sets, ints_ref, adjoint_ref, mine_ref, other_ref, total_ref)
    post(total_ref, *out_refs)


def last_kernel(sets, far_at, ints_ref, *refs):
    arrived, (keep_ref, send_ref, sum_ref) = refs[:5], refs[5:]
    collect(sets, far_at, ints_ref, *arrived, sum_ref)
    part = keep_ref.shape[0]
    core = ints_ref[far_at - 1]
    keep_ref[...] = sum_ref[pl.ds(pl.multiple_of(core * part, part), part), :].astype(BF16)
    send_ref[...] = sum_ref[pl.ds(pl.multiple_of((1 - core) * part, part), part), :].astype(BF16)


def place_kernel(sets, place_ref, keep_ref, recv_ref, out_ref):
    core = place_ref[0]
    width = keep_ref.shape[1]
    for half, ref in ((core, keep_ref), (1 - core, recv_ref)):
        rows = pl.ds(pl.multiple_of(half * sets, sets), sets)
        for block in range(keep_ref.shape[0] // sets):
            out_ref[rows, block * width : (block + 1) * width] = ref[block * sets : (block + 1) * sets, :]


def gradient_kernel(
    sets, tiles, ints_ref, own_ref, above_ref, below_ref, low_ref, high_ref, *refs
):
    columns, adjoints = refs[: STEPS - 1], refs[STEPS - 1 : 2 * STEPS - 1]
    mine_ref, other_ref, seen_ref, rows_ref, cols_ref = refs[2 * STEPS - 1 :]
    near = adjoints[0].shape[0]
    scale = 1.0 / (2 * sets)
    fill(near, low_ref.shape[0], own_ref, above_ref, below_ref, low_ref, high_ref, seen_ref)
    for t in range(STEPS):
        for block in range(near // sets):
            rows_ref[block, t * sets : (t + 1) * sets, :] = adjoints[t][block * sets : (block + 1) * sets, :]
    for i in range(2 * tiles):
        for t in range(STEPS - 1):
            cols_ref[t * sets : (t + 1) * sets, :] = columns[t][i * sets : (i + 1) * sets, :]
        cols_ref[(STEPS - 1) * sets :, :] = seen_ref[blocks(ints_ref[i], sets), :]
        product = lax.dot_general(
            rows_ref[ints_ref[2 * tiles + i]], cols_ref[...], (((0,), (0,)), ((), ())), preferred_element_type=F32
        )
        if i < tiles:
            mine_ref[i] = product * scale
        else:
            other_ref[i - tiles] = (product * scale).astype(BF16)


def portions_kernel(portion, place_ref, mine_ref, recv_ref, *out_refs):
    place, groups = place_ref[1], len(out_refs)
    for distance, out_ref in enumerate(out_refs):
        to = lax.rem(place + distance, groups)
        rows = pl.ds(pl.multiple_of(to * portion, portion), portion)
        total = mine_ref[:, rows, :] + recv_ref[:, rows, :].astype(F32)
        out_ref[...] = total.astype(out_ref.dtype)


def shards(tile_values, tile_row, tile_dest, trans_block, inj_pores, final_weight):
    tiles, width = tile_values.shape[:2]
    sets = final_weight.shape[0] // 2
    count = final_weight.shape[1] // width
    slots = trans_block.shape[1]
    capacity = slots // (NEIGH + 1)
    near, far = 2 * count * sets, capacity * sets
    core = lax.rem(lax.axis_index("blk"), 2).astype(I32)
    place = jnp.stack([core, lax.axis_index("inj").astype(I32)])

    other_core = 1 - core
    entries = inj_pores.shape[1]
    listed = jnp.concatenate([tile_row, tile_dest[:, 0], trans_block[0]])
    extra = -(-listed.shape[0] // entries)
    listed = jnp.pad(listed, (0, extra * entries - listed.shape[0]))
    other_ints = pair_swap(
        jnp.concatenate(
            [lax.dynamic_slice_in_dim(inj_pores, other_core * sets, sets, 0), listed.reshape(extra, entries)]
        )
    )
    other_weight = pair_swap(lax.dynamic_slice_in_dim(final_weight, other_core * sets, sets, 0))
    other_values = pair_swap(tile_values)
    listed, other_listed = listed[None, :], other_ints[sets:].reshape(1, -1)
    table_at = 2 * tiles
    tables = [one[0, table_at : table_at + slots] for one in (listed, other_listed)]
    table = jnp.where(core == 0, jnp.concatenate(tables), jnp.concatenate(tables[::-1]))
    sent_table = jnp.pad(table.astype(BF16), (0, 16 * width - 2 * slots)).reshape(16, width)

    def given_out(*sizes):
        return [shape(near, width, F32)] + [shape(rows, width) for rows in sizes]

    def give(above, below, low, high):
        from_low, from_high = far_pairs(high, low)
        return pair_shift(below, -1), pair_shift(above, 1), from_low, from_high

    def fetch(state, up, down):
        low, high = far_pairs(up, down)
        return pair_shift(state, -1), pair_shift(state, 1), low, high

    state, up, down = call(
        functools.partial(count_kernel, width, count, capacity, table_at), [place, listed, other_listed],
        [inj_pores, other_ints, sent_table],
        [shape(near + 16, width), shape(far, width), shape(far, width)],
        [pltpu.VMEM((2 * count, sets, width), F32)],
    )
    slot_rows = 4 * capacity * sets
    far_at = 4 * tiles + 1
    slots_at = far_at + 2 * capacity
    int_count = slots_at + 10 * capacity
    plan, weight, own, *posted = call(
        functools.partial(first_terms_kernel, sets, table_at), [place, listed, other_listed],
        [final_weight, other_weight, tile_values, other_values],
        [
            jax.ShapeDtypeStruct((int_count + 2 * tiles,), I32), shape(near, width),
            *given_out(slot_rows, slot_rows, far, far),
        ],
        [
            pltpu.SMEM((2 * (NEIGH + 1),), I32), pltpu.SMEM((4 * tiles,), I32),
            pltpu.VMEM((near + 2 * slot_rows + 2 * far, width), F32),
        ],
    )
    state, up, down, own = lax.optimization_barrier((state, up, down, own))
    given = give(*posted)
    arrived = fetch(state, up, down)
    tables = jnp.concatenate([table] + [block[near, : 2 * slots].astype(I32) for block in arrived[:2]])

    seen = pltpu.VMEM((3 * near + 2 * far, width), BF16)
    seen_sum = pltpu.VMEM((3 * near + 2 * far, width), F32)
    own_sum = pltpu.VMEM((near, width), F32)

    columns, adjoints = [], [weight]
    for step in range(STEPS - 1):
        outs = [shape(near, width), shape(far, width), shape(far, width), shape(2 * tiles * sets, width)]
        arrays = [state, *arrived, tile_values, other_values]
        if step == 0:
            ints, state, up, down, column_blocks = call(
                functools.partial(first_forward_kernel, sets, far_at, slots), [plan, tables], arrays,
                [jax.ShapeDtypeStruct((int_count,), I32), *outs], [seen, own_sum],
            )
        else:
            state, up, down, column_blocks = call(
                functools.partial(forward_kernel, sets, far_at), [ints], arrays, outs, [seen, own_sum]
            )
        columns.append(column_blocks)
        arrived = fetch(state, up, down)
        body = functools.partial(adjoint_kernel, sets, far_at)
        if step == 0:
            body = functools.partial(slots_adjoint_kernel, sets, slots_at)
        adjoint, own, *posted = call(
            body, [ints], [own, *given, tile_values, other_values],
            [shape(near, width), *given_out(near, near, far, far)], [seen_sum, own_sum],
        )
        adjoints.insert(0, adjoint)
        given = give(*posted)

    mine, other = call(
        functools.partial(gradient_kernel, sets, tiles), [ints], [state, *arrived, *columns, *adjoints],
        [jax.ShapeDtypeStruct((tiles, width, width), F32), jax.ShapeDtypeStruct((tiles, width, width), BF16)],
        [seen, pltpu.VMEM((2 * count, STEPS * sets, width), BF16), pltpu.VMEM((STEPS * sets, width), BF16)],
    )
    groups = lax.axis_size("inj")
    portion = width // groups
    pieces = call(
        functools.partial(portions_kernel, portion), [place], [mine, pair_swap(other)],
        [jax.ShapeDtypeStruct((tiles, portion, width), F32 if k == 0 else BF16) for k in range(groups)],
    )
    total = pieces[0]
    for distance in range(1, groups):
        route = [(i, (i + distance) % groups) for i in range(groups)]
        total = total + lax.ppermute(pieces[distance], "inj", route).astype(F32)

    keep, send = call(
        functools.partial(last_kernel, sets, far_at), [ints], [own, *given],
        [shape(near // 2, width), shape(near // 2, width)], [own_sum],
    )
    (sensitivity,) = call(
        functools.partial(place_kernel, sets), [place], [keep, pair_swap(send)],
        [shape(2 * sets, count * width)],
    )
    return sensitivity, total.astype(BF16)


def solution(mesh):
    placed = (
        P("blk", None, None),
        P("blk"),
        P("blk", None),
        P("blk", None),
        P("inj", "blk"),
        P("inj", "blk"),
    )
    return jax.shard_map(
        shards,
        mesh=mesh,
        in_specs=placed,
        out_specs=(P("inj", "blk"), P("blk", "inj", None)),
        check_vma=False,
    )
```

```python
import functools

import jax
import jax.numpy as jnp
from jax import lax
from jax.experimental import pallas as pl
from jax.experimental.pallas import tpu as pltpu
from jax.sharding import PartitionSpec as P

NEIGH = 6
STEPS = 4
F32, BF16, I32 = jnp.float32, jnp.bfloat16, jnp.int32


def pair_shift(block, amount):
    count = lax.axis_size("blk")
    return lax.ppermute(block, "blk", [(i, (i + 2 * amount) % count) for i in range(count)])


def pair_swap(block):
    return lax.ppermute(block, "blk", [(i, i ^ 1) for i in range(lax.axis_size("blk"))])


def far_pairs(block):
    if lax.axis_size("blk") == 8:
        return pair_shift(block, 2)
    half = block.shape[0] // 2
    return jnp.concatenate([pair_shift(block[:half], 2), pair_shift(block[half:], -2)])


def vmem():
    return pl.BlockSpec(memory_space=pltpu.VMEM)


def smem():
    return pl.BlockSpec(memory_space=pltpu.SMEM)


def call(body, ints, arrays, outs, scratch=()):
    return pl.pallas_call(
        body,
        out_shape=outs,
        in_specs=[smem()] * len(ints) + [vmem()] * len(arrays),
        out_specs=[smem() if out.dtype == I32 else vmem() for out in outs],
        scratch_shapes=list(scratch),
        compiler_params=pltpu.CompilerParams(vmem_limit_bytes=32 * 1024 * 1024),
    )(*ints, *arrays)


def shape(rows, width, kind=BF16):
    return jax.ShapeDtypeStruct((rows, width), kind)


def blocks(start, sets, count=1):
    return pl.ds(pl.multiple_of(start * sets, sets), sets * count)


def slot_of(offset):
    return 2 * offset - 1 if offset > 0 else -2 * offset


def read_table(core, mine_ref, other_ref, device, at):
    return jnp.where(core == device, mine_ref[0, at], other_ref[0, at])


def list_far(capacity, count, table_at, core, mine_ref, other_ref):
    return [
        read_table(core, mine_ref, other_ref, device, table_at + slot_of(offset) * capacity + k) + device * count
        for device, offset in ((1, -3), (0, 3))
        for k in range(capacity)
    ]


def count_kernel(
    width, count, capacity, table_at, place_ref, mine_ref, other_ref, pores_ref, recv_ref, table_ref,
    state_ref, far_ref, counts_ref,
):
    core = place_ref[0]
    sets, entries = pores_ref.shape[0] // 2, pores_ref.shape[1]
    rows = pl.ds(pl.multiple_of(core * sets, sets), sets)
    own = pores_ref[rows, :] + core * (count * width)
    pores = jnp.concatenate([own, recv_ref[:sets, :] + (1 - core) * (count * width)], axis=1)
    block = lax.div(pores, width)
    place = pores - block * width
    block_ids = lax.broadcasted_iota(I32, (2 * count, 2 * entries), 0)
    place_ids = lax.broadcasted_iota(I32, (width, 2 * entries), 0)
    for one in range(sets):
        row = slice(one, one + 1)
        by_block = jnp.where(block[row, :] == block_ids, 1.0, 0.0).astype(BF16)
        by_place = jnp.where(place[row, :] == place_ids, 1.0, 0.0).astype(BF16)
        counts_ref[:, one, :] = lax.dot_general(
            by_block, by_place, (((1,), (1,)), ((), ())), preferred_element_type=F32
        )
    for k in range(2 * count):
        state_ref[k * sets : (k + 1) * sets, :] = counts_ref[k].astype(BF16)
    state_ref[2 * count * sets :, :] = table_ref[...]
    pick_far(sets, list_far(capacity, count, table_at, core, mine_ref, other_ref), state_ref, far_ref)


def pick_far(sets, listed, state_ref, far_ref):
    for k, block in enumerate(listed):
        far_ref[k * sets : (k + 1) * sets, :] = state_ref[blocks(block, sets), :]


def fill(near, own_ref, above_ref, below_ref, far_ref, into_ref):
    into_ref[:near, :] = own_ref[:near, :]
    into_ref[near : 2 * near, :] = above_ref[:near, :]
    into_ref[2 * near : 3 * near, :] = below_ref[:near, :]
    into_ref[3 * near :, :] = far_ref[...]


def forward_kernel(
    sets, far_at, ints_ref, own_ref, above_ref, below_ref, beyond_ref, mine_ref, other_ref,
    state_ref, far_ref, columns_ref, seen_ref, total_ref,
):
    tiles = mine_ref.shape[0]
    fill(state_ref.shape[0], own_ref, above_ref, below_ref, beyond_ref, seen_ref)
    total_ref[...] = jnp.zeros_like(total_ref)
    for i in range(2 * tiles):
        tile = mine_ref[i] if i < tiles else other_ref[i - tiles]
        column = seen_ref[blocks(ints_ref[i], sets), :]
        columns_ref[i * sets : (i + 1) * sets, :] = column
        rows = blocks(ints_ref[2 * tiles + i], sets)
        total_ref[rows, :] += lax.dot_general(column, tile, (((1,), (1,)), ((), ())), preferred_element_type=F32)
    state_ref[...] = total_ref[...].astype(BF16)
    pick_far(sets, [ints_ref[far_at + k] for k in range(far_ref.shape[0] // sets)], state_ref, far_ref)


def first_forward_kernel(sets, far_at, slots, plan_ref, tables_ref, *refs):
    arrays, ints_ref, rest = refs[:6], refs[6], refs[7:]
    tiles, near = arrays[-1].shape[0], rest[0].shape[0]
    count = near // sets // 2
    for i in range(2 * tiles):
        side, at = plan_ref[i], plan_ref[2 * tiles + i]
        listed = side * count + tables_ref[jnp.minimum(side, 5) * slots + at]
        ints_ref[i] = jnp.where(side == 6, 6 * count + at, listed)
    for k in range(2 * tiles, ints_ref.shape[0]):
        ints_ref[k] = plan_ref[2 * tiles + k]
    forward_kernel(sets, far_at, ints_ref, *arrays, *rest)


def terms(sets, ints_ref, adjoint_ref, mine_ref, other_ref, total_ref):
    tiles = mine_ref.shape[0]
    total_ref[...] = jnp.zeros_like(total_ref)
    for i in range(2 * tiles):
        tile = mine_ref[i] if i < tiles else other_ref[i - tiles]
        row = adjoint_ref[blocks(ints_ref[2 * tiles + i], sets), :]
        total_ref[blocks(ints_ref[i], sets), :] += jnp.dot(row, tile, preferred_element_type=F32)


def post(total_ref, own_ref, above_ref, below_ref, far_ref):
    at, half = own_ref.shape[0], far_ref.shape[0] // 2
    own_ref[...] = total_ref[:at, :]
    for ref in (above_ref, below_ref):
        ref[...] = total_ref[at : at + ref.shape[0], :].astype(BF16)
        at += ref.shape[0]
    far_ref[half:, :] = total_ref[at : at + half, :].astype(BF16)
    far_ref[:half, :] = total_ref[at + half :, :].astype(BF16)


def collect(sets, far_at, ints_ref, own_ref, above_ref, below_ref, far_ref, sum_ref):
    sum_ref[...] = own_ref[...] + above_ref[...].astype(F32) + below_ref[...].astype(F32)
    slots = far_ref.shape[0] // sets
    for k in range(slots):
        block = ints_ref[far_at + (k + slots // 2) % slots]
        sum_ref[blocks(block, sets), :] += far_ref[k * sets : (k + 1) * sets, :].astype(F32)


def first_terms_kernel(
    sets, table_at, place_ref, listed_ref, arrived_ref, weight_ref, recv_ref, mine_ref, other_ref,
    plan_ref, placed_ref, *rest,
):
    *out_refs, used_ref, ints_ref, total_ref = rest
    core, width, tiles = place_ref[0], placed_ref.shape[1], mine_ref.shape[0]
    count = weight_ref.shape[1] // width
    capacity = out_refs[-1].shape[0] // sets // 2
    rows = pl.ds(pl.multiple_of(core * sets, sets), sets)
    for block in range(count):
        lanes = slice(block * width, (block + 1) * width)
        placed_ref[blocks(core * count + block, sets), :] = weight_ref[rows, lanes]
        placed_ref[blocks((1 - core) * count + block, sets), :] = recv_ref[:, lanes]
    for k in range(2 * (NEIGH + 1)):
        used_ref[k] = 0
    for i in range(2 * tiles):
        mine = i < tiles
        owner, from_ref, at = (core, listed_ref, i) if mine else (1 - core, arrived_ref, i - tiles)
        target = from_ref[0, tiles + at]
        used_at = target + (0 if mine else NEIGH + 1)
        position = used_ref[used_at]
        used_ref[used_at] = position + 1
        half = lax.shift_right_logical(target + 1, 1)
        reach = owner + jnp.where(target & 1 == 1, half, -half)
        pair_off = lax.shift_right_logical(reach + 4, 1) - 2
        parity = reach - 2 * pair_off
        far = (pair_off == 2) | (pair_off == -2)
        far_slot = jnp.where(pair_off == 2, capacity, 0) + position
        source = jnp.where(pair_off == -1, 2, pair_off)
        entry = target * capacity + position
        own = parity * count + read_table(core, listed_ref, arrived_ref, parity, table_at + entry)
        slot = 2 * count + ((source - 1) * 4 + owner * 2 + parity) * capacity + position
        ints_ref[i] = jnp.where(far, 2 * count + 8 * capacity + far_slot, jnp.where(pair_off == 0, own, slot))
        row = owner * count + from_ref[0, at]
        ints_ref[2 * tiles + i] = row
        plan_ref[i] = jnp.where(far, 6, source * 2 + parity)
        plan_ref[2 * tiles + i] = jnp.where(far, far_slot, entry)
        plan_ref[4 * tiles + i] = row
    plan_ref[6 * tiles] = core
    far_blocks = list_far(capacity, count, table_at, core, listed_ref, arrived_ref)
    slot_blocks = [
        read_table(core, listed_ref, arrived_ref, device, table_at + slot_of(2 * side + device - sender) * capacity + k)
        + device * count
        for side in (-1, 1)
        for sender in (0, 1)
        for device in (0, 1)
        for k in range(capacity)
    ]
    for k, block in enumerate(far_blocks + slot_blocks + far_blocks[capacity:] + far_blocks[:capacity]):
        plan_ref[6 * tiles + 1 + k] = block
    terms(sets, ints_ref, placed_ref, mine_ref, other_ref, total_ref)
    post(total_ref, *out_refs)


def slots_adjoint_kernel(sets, slots_at, ints_ref, *refs):
    (own_ref, *arrived), (mine_ref, other_ref, adjoint_ref), rest = refs[:4], refs[4:7], refs[7:]
    *out_refs, total_ref, sum_ref = rest
    sum_ref[...] = own_ref[...]
    at = slots_at
    for ref in arrived:
        for k in range(ref.shape[0] // sets):
            sum_ref[blocks(ints_ref[at], sets), :] += ref[k * sets : (k + 1) * sets, :].astype(F32)
            at += 1
    adjoint_ref[...] = sum_ref[...].astype(BF16)
    terms(sets, ints_ref, adjoint_ref, mine_ref, other_ref, total_ref)
    post(total_ref, *out_refs)


def adjoint_kernel(sets, far_at, ints_ref, *refs):
    arrived, (mine_ref, other_ref, adjoint_ref), rest = refs[:4], refs[4:7], refs[7:]
    *out_refs, total_ref, sum_ref = rest
    collect(sets, far_at, ints_ref, *arrived, sum_ref)
    adjoint_ref[...] = sum_ref[...].astype(BF16)
    terms(sets, ints_ref, adjoint_ref, mine_ref, other_ref, total_ref)
    post(total_ref, *out_refs)


def last_kernel(sets, far_at, ints_ref, *refs):
    arrived, (keep_ref, send_ref, sum_ref) = refs[:4], refs[4:]
    collect(sets, far_at, ints_ref, *arrived, sum_ref)
    part = keep_ref.shape[0]
    core = ints_ref[far_at - 1]
    keep_ref[...] = sum_ref[pl.ds(pl.multiple_of(core * part, part), part), :].astype(BF16)
    send_ref[...] = sum_ref[pl.ds(pl.multiple_of((1 - core) * part, part), part), :].astype(BF16)


def place_kernel(sets, place_ref, keep_ref, recv_ref, out_ref):
    core = place_ref[0]
    width = keep_ref.shape[1]
    for half, ref in ((core, keep_ref), (1 - core, recv_ref)):
        rows = pl.ds(pl.multiple_of(half * sets, sets), sets)
        for block in range(keep_ref.shape[0] // sets):
            out_ref[rows, block * width : (block + 1) * width] = ref[block * sets : (block + 1) * sets, :]


def gradient_kernel(
    sets, tiles, ints_ref, own_ref, above_ref, below_ref, far_ref, *refs
):
    columns, adjoints = refs[: STEPS - 1], refs[STEPS - 1 : 2 * STEPS - 1]
    mine_ref, other_ref, seen_ref, rows_ref, cols_ref = refs[2 * STEPS - 1 :]
    near = adjoints[0].shape[0]
    scale = 1.0 / (2 * sets)
    fill(near, own_ref, above_ref, below_ref, far_ref, seen_ref)
    for t in range(STEPS):
        for block in range(near // sets):
            rows_ref[block, t * sets : (t + 1) * sets, :] = adjoints[t][block * sets : (block + 1) * sets, :]
    for i in range(2 * tiles):
        for t in range(STEPS - 1):
            cols_ref[t * sets : (t + 1) * sets, :] = columns[t][i * sets : (i + 1) * sets, :]
        cols_ref[(STEPS - 1) * sets :, :] = seen_ref[blocks(ints_ref[i], sets), :]
        product = lax.dot_general(
            rows_ref[ints_ref[2 * tiles + i]], cols_ref[...], (((0,), (0,)), ((), ())), preferred_element_type=F32
        )
        if i < tiles:
            mine_ref[i] = product * scale
        else:
            other_ref[i - tiles] = (product * scale).astype(BF16)


def portions_kernel(portion, place_ref, mine_ref, recv_ref, *out_refs):
    place, groups = place_ref[1], len(out_refs)
    for distance, out_ref in enumerate(out_refs):
        to = lax.rem(place + distance, groups)
        rows = pl.ds(pl.multiple_of(to * portion, portion), portion)
        total = mine_ref[:, rows, :] + recv_ref[:, rows, :].astype(F32)
        out_ref[...] = total.astype(out_ref.dtype)


def shards(tile_values, tile_row, tile_dest, trans_block, inj_pores, final_weight):
    tiles, width = tile_values.shape[:2]
    sets = final_weight.shape[0] // 2
    count = final_weight.shape[1] // width
    slots = trans_block.shape[1]
    capacity = slots // (NEIGH + 1)
    near, far = 2 * count * sets, 2 * capacity * sets
    core = lax.rem(lax.axis_index("blk"), 2).astype(I32)
    place = jnp.stack([core, lax.axis_index("inj").astype(I32)])

    other_core = 1 - core
    entries = inj_pores.shape[1]
    listed = jnp.concatenate([tile_row, tile_dest[:, 0], trans_block[0]])
    extra = -(-listed.shape[0] // entries)
    listed = jnp.pad(listed, (0, extra * entries - listed.shape[0]))
    other_ints = pair_swap(
        jnp.concatenate(
            [lax.dynamic_slice_in_dim(inj_pores, other_core * sets, sets, 0), listed.reshape(extra, entries)]
        )
    )
    other_weight = pair_swap(lax.dynamic_slice_in_dim(final_weight, other_core * sets, sets, 0))
    other_values = pair_swap(tile_values)
    listed, other_listed = listed[None, :], other_ints[sets:].reshape(1, -1)
    table_at = 2 * tiles
    tables = [one[0, table_at : table_at + slots] for one in (listed, other_listed)]
    table = jnp.where(core == 0, jnp.concatenate(tables), jnp.concatenate(tables[::-1]))
    sent_table = jnp.pad(table.astype(BF16), (0, 16 * width - 2 * slots)).reshape(16, width)

    def given_out(*sizes):
        return [shape(near, width, F32)] + [shape(rows, width) for rows in sizes]

    def give(above, below, beyond):
        from_far = far_pairs(beyond)
        return pair_shift(below, -1), pair_shift(above, 1), from_far

    def fetch(state, beyond):
        from_far = far_pairs(beyond)
        return pair_shift(state, -1), pair_shift(state, 1), from_far

    state, beyond = call(
        functools.partial(count_kernel, width, count, capacity, table_at), [place, listed, other_listed],
        [inj_pores, other_ints, sent_table],
        [shape(near + 16, width), shape(far, width)],
        [pltpu.VMEM((2 * count, sets, width), F32)],
    )
    slot_rows = 4 * capacity * sets
    far_at = 4 * tiles + 1
    slots_at = far_at + 2 * capacity
    int_count = slots_at + 10 * capacity
    plan, weight, own, *posted = call(
        functools.partial(first_terms_kernel, sets, table_at), [place, listed, other_listed],
        [final_weight, other_weight, tile_values, other_values],
        [
            jax.ShapeDtypeStruct((int_count + 2 * tiles,), I32), shape(near, width),
            *given_out(slot_rows, slot_rows, far),
        ],
        [
            pltpu.SMEM((2 * (NEIGH + 1),), I32), pltpu.SMEM((4 * tiles,), I32),
            pltpu.VMEM((near + 2 * slot_rows + far, width), F32),
        ],
    )
    state, beyond, own = lax.optimization_barrier((state, beyond, own))
    given = give(*posted)
    arrived = fetch(state, beyond)
    tables = jnp.concatenate([table] + [block[near, : 2 * slots].astype(I32) for block in arrived[:2]])

    seen = pltpu.VMEM((3 * near + far, width), BF16)
    seen_sum = pltpu.VMEM((3 * near + far, width), F32)
    own_sum = pltpu.VMEM((near, width), F32)

    columns, adjoints = [], [weight]
    for step in range(STEPS - 1):
        outs = [shape(near, width), shape(far, width), shape(2 * tiles * sets, width)]
        arrays = [state, *arrived, tile_values, other_values]
        if step == 0:
            ints, state, beyond, column_blocks = call(
                functools.partial(first_forward_kernel, sets, far_at, slots), [plan, tables], arrays,
                [jax.ShapeDtypeStruct((int_count,), I32), *outs], [seen, own_sum],
            )
        else:
            state, beyond, column_blocks = call(
                functools.partial(forward_kernel, sets, far_at), [ints], arrays, outs, [seen, own_sum]
            )
        columns.append(column_blocks)
        arrived = fetch(state, beyond)
        body = functools.partial(adjoint_kernel, sets, far_at)
        if step == 0:
            body = functools.partial(slots_adjoint_kernel, sets, slots_at)
        adjoint, own, *posted = call(
            body, [ints], [own, *given, tile_values, other_values],
            [shape(near, width), *given_out(near, near, far)], [seen_sum, own_sum],
        )
        adjoints.insert(0, adjoint)
        given = give(*posted)

    mine, other = call(
        functools.partial(gradient_kernel, sets, tiles), [ints], [state, *arrived, *columns, *adjoints],
        [jax.ShapeDtypeStruct((tiles, width, width), F32), jax.ShapeDtypeStruct((tiles, width, width), BF16)],
        [seen, pltpu.VMEM((2 * count, STEPS * sets, width), BF16), pltpu.VMEM((STEPS * sets, width), BF16)],
    )
    groups = lax.axis_size("inj")
    portion = width // groups
    pieces = call(
        functools.partial(portions_kernel, portion), [place], [mine, pair_swap(other)],
        [jax.ShapeDtypeStruct((tiles, portion, width), F32 if k == 0 else BF16) for k in range(groups)],
    )
    total = pieces[0]
    for distance in range(1, groups):
        route = [(i, (i + distance) % groups) for i in range(groups)]
        total = total + lax.ppermute(pieces[distance], "inj", route).astype(F32)

    keep, send = call(
        functools.partial(last_kernel, sets, far_at), [ints], [own, *given],
        [shape(near // 2, width), shape(near // 2, width)], [own_sum],
    )
    (sensitivity,) = call(
        functools.partial(place_kernel, sets), [place], [keep, pair_swap(send)],
        [shape(2 * sets, count * width)],
    )
    return sensitivity, total.astype(BF16)


def solution(mesh):
    placed = (
        P("blk", None, None),
        P("blk"),
        P("blk", None),
        P("blk", None),
        P("inj", "blk"),
        P("inj", "blk"),
    )
    return jax.shard_map(
        shards,
        mesh=mesh,
        in_specs=placed,
        out_specs=(P("inj", "blk"), P("blk", "inj", None)),
        check_vma=False,
    )
```
